32 devices in a mesh: video: 2 (over x), seq: 8 (over z, y), head: 2 (over core).
Axes of the slice: x: 2, y: 2, z: 4, core: 2. Of those that a mesh axis runs over, the one named last changes fastest.
Arguments:
- query: bfloat16 [6144, 1536], P(('video', 'seq'), 'head'), parts along dimension 0, may hold values from -5 to 5
- key: bfloat16 [6144, 1536], P(('video', 'seq'), 'head'), parts along dimension 0, may hold values from -5 to 5
- value: bfloat16 [6144, 1536], P(('video', 'seq'), 'head'), parts along dimension 0, may hold values from -6 to 6
- stream: bfloat16 [6144, 3072], P(('video', 'seq'), 'head'), parts along dimension 0, may hold values from -12 to 12
- shift_mod: float32 [6144], P('video'), parts along dimension 0, may hold values from -3 to 3
- scale_mod: float32 [6144], P('video'), parts along dimension 0, may hold values from -3 to 3
- out_weight: bfloat16 [1536, 3072], P('seq', 'head'), may hold values from -0.5 to 0.5
Outputs:
- normed: bfloat16 [6144, 3072], P(('video', 'seq'), 'head'), parts along dimension 0
- stream_out: bfloat16 [6144, 3072], P(('video', 'seq'), 'head'), parts along dimension 0
The draws below stay inside these ranges and needn't reach their ends.
There are 2 independent parts, one for each index of `video`. The reference program is written for one: setup_inputs(seed, part) draws one part's arguments, and reference() takes and returns one part's arrays. A program takes and returns all parts, laid end to end along the dimension named above; an argument that names none is the same for every part. Nothing has to cross between parts.
All inputs are finite; a program needn't handle non-finite values.
Results may differ from the reference program's by a relative error of at most 0.0051.
Values may be sent and summed in bfloat16 or wider, within the bound.
A program may use at most 128 MiB of HBM per device.

```python
import math
import jax
import jax.numpy as jnp
from jax import lax

D = 3072
HEADS = 12
HD = 128
TILE = 128
WT = 3
HT = 4
TT = 2
TOKENS = 3072


def drawn_pair(key):
    features = HEADS * HD
    base_query = jnp.clip(1.2 * jax.random.normal(jax.random.fold_in(key, 101), (TOKENS, features), jnp.float32), -4.8, 4.8)
    base_key = jnp.clip(1.2 * jax.random.normal(jax.random.fold_in(key, 102), (TOKENS, features), jnp.float32), -4.8, 4.8)
    return (base_query, base_key)


def draw_query(key, part):
    return drawn_pair(key)[0].astype(jnp.bfloat16)


def draw_key(key, part):
    return drawn_pair(key)[1].astype(jnp.bfloat16)


def draw_stream(key, part):
    base = jnp.clip(jax.random.normal(jax.random.fold_in(key, 201), (TOKENS, D), jnp.float32), -4.0, 4.0)
    column_ramp = 1.0 + 2.0 * jnp.arange(D, dtype=jnp.float32) / D
    column_scale = jnp.exp(jax.random.uniform(jax.random.fold_in(key, 202), (D,), jnp.float32, math.log(0.05), 0.0)) * column_ramp
    row_scale = jnp.exp(jax.random.uniform(jax.random.fold_in(key, 203), (TOKENS,), jnp.float32, math.log(0.2), 0.0))
    return (base * column_scale[None, :] * row_scale[:, None]).astype(jnp.bfloat16)


def steps_of(rng, dims, split, low, high):
    def one(axis_at, parts):
        steps = jax.random.uniform(jax.random.fold_in(jax.random.fold_in(rng, 6), axis_at), (parts,), jnp.float32, low / len(split), high / len(split))
        return jnp.repeat(jnp.exp(steps), dims[axis_at] // parts).reshape((-1,) + (1,) * (len(dims) - axis_at - 1))

    loudness = one(*split[0])
    for cut in split[1:]:
        loudness = loudness * one(*cut)
    return loudness


def noise(own_key, dims, scale, limit, shards=(), kind=jnp.bfloat16):
    level = steps_of(own_key, dims, shards, -0.22, 0.18) if shards else 1.0
    entries = jax.random.normal(own_key, dims, jnp.float32) * scale * level
    return jnp.minimum(jnp.maximum(entries, -limit), limit).astype(kind)


def setup_inputs(seed: int = 0, part: int = 0) -> dict:
    arg_keys = jax.random.split(jax.random.key(seed), 8)
    part_splits = jax.random.split(jax.random.fold_in(arg_keys[7], part), 8)
    return {
        "query": draw_query(jax.random.fold_in(jax.random.fold_in(arg_keys[7], part), 71), part),
        "key": draw_key(jax.random.fold_in(jax.random.fold_in(arg_keys[7], part), 71), part),
        "value": noise(part_splits[2], (TOKENS, HEADS * HD), 1.0, 6.0, ((0, 8), (1, 2))),
        "stream": draw_stream(jax.random.fold_in(jax.random.fold_in(arg_keys[7], part), 71), part),
        "shift_mod": noise(part_splits[4], (D,), 0.5, 3.0, (), jnp.float32),
        "scale_mod": noise(part_splits[5], (D,), 0.5, 3.0, (), jnp.float32),
        "out_weight": noise(arg_keys[6], (HEADS * HD, D), HD ** -0.5, 0.5, ((0, 8), (1, 2))),
    }


def reference(query, key, value, stream, shift_mod, scale_mod, out_weight):
    slab = WT * TILE
    layer_rows = HT * slab
    shape_four = (TT, layer_rows, HEADS, HD)
    padding = ((1, 1), (0, 0), (0, 0), (0, 0))
    query_layers = query.reshape(shape_four)
    key_layers = jnp.pad(key.reshape(shape_four), padding)
    value_layers = jnp.pad(value.reshape(shape_four), padding)
    rows = jnp.arange(layer_rows, dtype=jnp.int32)
    height = rows // slab
    width = rows // TILE % WT
    key_height = jnp.tile(height, 3)
    key_width = jnp.tile(width, 3)
    near = (jnp.abs(height[:, None] - key_height[None, :]) <= 1) & (jnp.abs(width[:, None] - key_width[None, :]) <= 1)

    def one_layer(layer):
        queries = lax.dynamic_index_in_dim(query_layers, layer, 0, keepdims=False).astype(jnp.float32)
        keys_here = lax.dynamic_slice_in_dim(key_layers, layer, 3, 0).reshape(3 * layer_rows, HEADS, HD).astype(jnp.float32)
        values_here = lax.dynamic_slice_in_dim(value_layers, layer, 3, 0).reshape(3 * layer_rows, HEADS, HD).astype(jnp.float32)
        key_time = layer - 1 + jnp.arange(3 * layer_rows, dtype=jnp.int32) // layer_rows
        visible = near & ((key_time >= 0) & (key_time < TT))[None, :]

        def one_head(head):
            head_query = lax.dynamic_index_in_dim(queries, head, 1, keepdims=False)
            head_key = lax.dynamic_index_in_dim(keys_here, head, 1, keepdims=False)
            head_value = lax.dynamic_index_in_dim(values_here, head, 1, keepdims=False)
            scores = jnp.dot(head_query, head_key.T, preferred_element_type=jnp.float32) / math.sqrt(HD)
            scores = jnp.where(visible, scores, -jnp.inf)
            top = lax.optimization_barrier(jnp.max(scores, axis=1, keepdims=True))
            expo = jnp.exp(scores - top)
            total = lax.optimization_barrier(jnp.sum(expo, axis=1, keepdims=True))
            probs = lax.optimization_barrier(expo.astype(jnp.bfloat16)).astype(jnp.float32)
            weighted = jnp.dot(probs, head_value, preferred_element_type=jnp.float32)
            return (weighted / total).astype(jnp.bfloat16)
        per_head = lax.map(one_head, jnp.arange(HEADS, dtype=jnp.int32))
        return jnp.transpose(per_head, (1, 0, 2))
    attended = lax.map(one_layer, jnp.arange(TT, dtype=jnp.int32)).reshape(TOKENS, HEADS * HD)
    mixed = stream.astype(jnp.float32) + jnp.dot(attended, out_weight, preferred_element_type=jnp.float32)
    mean = lax.optimization_barrier(jnp.mean(mixed, axis=1, keepdims=True))
    centered = mixed - mean
    var = lax.optimization_barrier(jnp.mean(centered * centered, axis=1, keepdims=True))
    normed = (centered * lax.rsqrt(var + 1e-06) * (1.0 + scale_mod) + shift_mod).astype(jnp.bfloat16)
    return (normed, mixed.astype(jnp.bfloat16))
```

```python
import functools
import math

import jax
import jax.numpy as jnp
from jax import lax
from jax.experimental import pallas as pl
from jax.experimental.pallas import tpu as pltpu
from jax.sharding import PartitionSpec as P

HD = 128
TILE = 128
HT = 4
MESH = pl.DeviceIdType.MESH
F32 = jnp.float32
BF16 = jnp.bfloat16


def attention_kernel(
    layers, spans, chunk, q_ref, k_ref, v_ref, out_ref,
    kbuf, vbuf, q_t, acc, top, total, send_sem, recv_sem, att_send, att_recv,
):
    rows, features = q_ref.shape
    chunks = features // chunk
    heads_chunk = chunk // HD
    width_tiles = rows // TILE
    position = lax.axis_index("seq")
    core = lax.axis_index("head")
    time = position // HT
    height = position % HT
    base = time * HT
    edge = (height == 0) | (height == HT - 1)
    inner = jnp.logical_not(edge)
    partner = base + height + 1 - 2 * (height % 2)
    far = base + (height + 2) % HT
    links = []
    if layers == 2:
        links.append((1, position + HT - 2 * base, True, True))
    elif layers > 2:
        links.append((1, position - HT, time > 0, time < layers - 1))
        links.append((2, position + HT, time < layers - 1, time > 0))

    def guarded(condition, body):
        if condition is True:
            body()
        else:
            pl.when(condition)(body)

    barrier = pltpu.get_barrier_semaphore()

    def greet(device):
        pl.semaphore_signal(barrier, inc=1, device_id=device, device_id_type=MESH)

    greet({"seq": partner})
    greet({"seq": far})
    greet({"head": 1 - core})
    peers = 3
    for _, target, sends, _ in links:
        guarded(sends, lambda target=target: greet({"seq": target}))
        peers = peers + (1 if sends is True else jnp.where(sends, 1, 0))
    pl.semaphore_wait(barrier, peers)

    def cols(c):
        return pl.ds(pl.multiple_of(c * chunk, chunk), chunk)

    def copies(span, hop, c, target):
        pair = []
        for which, (own, buf) in enumerate(((k_ref, kbuf), (v_ref, vbuf))):
            dst = buf.at[span, hop, :, cols(c)]
            if hop == 2:
                src = buf.at[span, 1, :, cols(c)]
            elif hop == 1 and span > 0:
                src = buf.at[span, 0, :, cols(c)]
            else:
                src = own.at[:, cols(c)]
            pair.append(pltpu.make_async_remote_copy(
                src_ref=src, dst_ref=dst,
                send_sem=send_sem.at[which, span, hop, c],
                recv_sem=recv_sem.at[which, span, hop, c],
                device_id={"seq": target}, device_id_type=MESH,
            ))
        return pair

    def start(span, hop, c, target):
        for copy in copies(span, hop, c, target):
            copy.start()

    def arrived(span, hop, c):
        for copy in copies(span, hop, c, partner):
            copy.wait_recv()

    def sent(span, hop, c, target):
        for copy in copies(span, hop, c, target):
            copy.wait_send()

    def first_sends(c, carry):
        for span, target, sends, _ in links:
            guarded(sends, lambda span=span, target=target: start(span, 0, c, target))
        start(0, 1, c, partner)
        return carry

    lax.fori_loop(0, chunks, first_sends, 0)

    for head in range(features // HD):
        q_t[head] = q_ref[:, head * HD : (head + 1) * HD].astype(F32).T.astype(BF16)
    acc[...] = jnp.zeros_like(acc)
    total[...] = jnp.zeros_like(total)
    top[...] = jnp.full_like(top, -jnp.inf)
    factor = math.log2(math.e) / math.sqrt(HD)

    def attend(keys, values, c):
        def one_head(index, carry):
            head = c * heads_chunk + index
            here = pl.ds(pl.multiple_of(head * HD, HD), HD)
            scores = jnp.dot(keys[:, here], q_t[head], preferred_element_type=F32)
            old = top[head]
            parts, news, sums = [], [], []
            for tile in range(width_tiles):
                low = max(tile - 1, 0) * TILE
                high = min(tile + 2, width_tiles) * TILE
                at = slice(tile * TILE, (tile + 1) * TILE)
                seen = scores[low:high, at] * factor
                new = jnp.maximum(jnp.max(seen, axis=0, keepdims=True), old[:, at])
                expo = jnp.exp2(seen - new)
                sums.append(jnp.sum(expo, axis=0, keepdims=True))
                news.append(new)
                column = [expo.astype(BF16)]
                if low > 0:
                    column.insert(0, jnp.zeros((low, TILE), BF16))
                if high < rows:
                    column.append(jnp.zeros((rows - high, TILE), BF16))
                parts.append(jnp.concatenate(column, 0) if len(column) > 1 else column[0])
            probs = jnp.concatenate(parts, 1)
            new = jnp.concatenate(news, 1)
            scale = jnp.exp2(old - new)
            top[head] = new
            total[head] = total[head] * scale + jnp.concatenate(sums, 1)
            weighted = lax.dot_general(
                values[:, here], probs, (((0,), (0,)), ((), ())), preferred_element_type=F32
            )
            acc[head] = acc[head] * scale + weighted
            return carry

        lax.fori_loop(0, heads_chunk, one_head, 0)

    def attend_slot(span, hop, c):
        attend(kbuf.at[span, hop], vbuf.at[span, hop], c)

    def own_block(c, carry):
        attend(k_ref, v_ref, c)
        return carry

    lax.fori_loop(0, chunks, own_block, 0)

    valid = [(0, True)] + [(span, has) for span, _, _, has in links]

    def far_blocks(c):
        for span, has in valid:
            def body(span=span):
                arrived(span, 2, c)
                attend_slot(span, 2, c)
            guarded(inner if has is True else inner & has, body)

    def step(c, carry):
        arrived(0, 1, c)
        pl.when(edge)(lambda: start(0, 2, c, far))
        for span, has in valid[1:]:
            def body(span=span):
                arrived(span, 0, c)
                start(span, 1, c, partner)
            guarded(has, body)
        attend_slot(0, 1, c)
        for span, has in valid[1:]:
            guarded(has, lambda span=span: attend_slot(span, 0, c))
        for span, has in valid[1:]:
            def body(span=span):
                arrived(span, 1, c)
                pl.when(edge)(lambda: start(span, 2, c, far))
                attend_slot(span, 1, c)
            guarded(has, body)
        pl.when(c > 0)(lambda: far_blocks(c - 1))
        return carry

    lax.fori_loop(0, chunks, step, 0)
    far_blocks(chunks - 1)

    for head in range(features // HD):
        done = acc[head] / total[head]
        out_ref[core, :, head * HD : (head + 1) * HD] = done.T.astype(BF16)
    across = pltpu.make_async_remote_copy(
        src_ref=out_ref.at[core], dst_ref=out_ref.at[core],
        send_sem=att_send, recv_sem=att_recv,
        device_id={"head": 1 - core}, device_id_type=MESH,
    )
    across.start()

    def drain(c, carry):
        for span, target, sends, _ in links:
            guarded(sends, lambda span=span, target=target: sent(span, 0, c, target))
        for span, has in valid:
            def body(span=span):
                sent(span, 1, c, partner)
                pl.when(edge)(lambda: sent(span, 2, c, far))
            guarded(has, body)
        return carry

    lax.fori_loop(0, chunks, drain, 0)
    across.wait_send()
    arrive = pltpu.make_async_remote_copy(
        src_ref=out_ref.at[1 - core], dst_ref=out_ref.at[1 - core],
        send_sem=att_send, recv_sem=att_recv,
        device_id={"head": 1 - core}, device_id_type=MESH,
    )
    arrive.wait_recv()


def attention(query, key, value, layers, heads_axis):
    rows, features = query.shape
    heads = features // HD
    chunk = 2 * HD if heads % 2 == 0 else HD
    chunks = features // chunk
    spans = min(layers, 3)
    vmem = pl.BlockSpec(memory_space=pltpu.VMEM)
    return pl.pallas_call(
        functools.partial(attention_kernel, layers, spans, chunk),
        out_shape=jax.ShapeDtypeStruct((heads_axis, rows, features), BF16),
        in_specs=[vmem] * 3,
        out_specs=vmem,
        scratch_shapes=[
            pltpu.VMEM((spans, 3, rows, features), BF16),
            pltpu.VMEM((spans, 3, rows, features), BF16),
            pltpu.VMEM((heads, HD, rows), BF16),
            pltpu.VMEM((heads, HD, rows), F32),
            pltpu.VMEM((heads, 1, rows), F32),
            pltpu.VMEM((heads, 1, rows), F32),
            pltpu.SemaphoreType.DMA((2, spans, 3, chunks)),
            pltpu.SemaphoreType.DMA((2, spans, 3, chunks)),
            pltpu.SemaphoreType.DMA,
            pltpu.SemaphoreType.DMA,
        ],
        compiler_params=pltpu.CompilerParams(
            collective_id=0, has_side_effects=True, vmem_limit_bytes=40 * 1024 * 1024
        ),
        cost_estimate=pl.CostEstimate(
            flops=4 * spans * 3 * rows * rows * features,
            bytes_accessed=100_000_000,
            transcendentals=spans * 3 * rows * rows * heads,
        ),
        name="tile_attention",
    )(query, key, value)


def project_kernel(
    width, att_ref, weight_ref, stream_ref, shift_ref, scale_ref, normed_ref, stream_out_ref,
    mixed, mine, theirs, send_sem, recv_sem,
):
    rows, columns = stream_ref.shape
    parts, _, depth = att_ref.shape
    core = lax.axis_index("head")
    other = {"head": 1 - core}
    barrier = pltpu.get_barrier_semaphore()
    pl.semaphore_signal(barrier, inc=1, device_id=other, device_id_type=MESH)
    step = 2 * HD
    sums = jnp.zeros((rows, HD), F32)
    squares = jnp.zeros((rows, HD), F32)
    for begin in range(0, columns, step):
        at = slice(begin, begin + step)
        block = stream_ref[:, at].astype(F32)
        product = jnp.dot(att_ref[0], weight_ref[0:depth, at], preferred_element_type=F32)
        for part in range(1, parts):
            product += jnp.dot(
                att_ref[part], weight_ref[part * depth : (part + 1) * depth, at],
                preferred_element_type=F32,
            )
        block = block + product
        mixed[:, at] = block
        stream_out_ref[:, at] = block.astype(BF16)
        for inside in range(0, step, HD):
            piece = block[:, inside : inside + HD]
            sums += piece
            squares += piece * piece
    lane = lax.broadcasted_iota(jnp.int32, (rows, HD), 1)
    sum_here = jnp.sum(sums, axis=1, keepdims=True)
    square_here = jnp.sum(squares, axis=1, keepdims=True)
    mine[...] = jnp.where(lane < HD // 2, sum_here, square_here)
    pl.semaphore_wait(barrier, 1)
    copy = pltpu.make_async_remote_copy(
        src_ref=mine, dst_ref=theirs, send_sem=send_sem, recv_sem=recv_sem,
        device_id=other, device_id_type=MESH,
    )
    copy.start()
    copy.wait()
    both = theirs[...]
    mean = (sum_here + both[:, 0:1]) / width
    var = (square_here + both[:, HD - 1 : HD]) / width - mean * mean
    inverse = lax.rsqrt(var + 1e-06)
    for begin in range(0, columns, step):
        at = slice(begin, begin + step)
        here = pl.ds(pl.multiple_of(core * columns + begin, step), step)
        gain = 1.0 + scale_ref[:, here]
        normed_ref[:, at] = (
            (mixed[:, at] - mean) * inverse * gain + shift_ref[:, here]
        ).astype(BF16)


def project(att, weight, stream, shift_mod, scale_mod):
    rows, columns = stream.shape
    width = shift_mod.shape[1]
    vmem = pl.BlockSpec(memory_space=pltpu.VMEM)
    return pl.pallas_call(
        functools.partial(project_kernel, width),
        out_shape=(
            jax.ShapeDtypeStruct((rows, columns), BF16),
            jax.ShapeDtypeStruct((rows, columns), BF16),
        ),
        in_specs=[vmem] * 5,
        out_specs=(vmem, vmem),
        scratch_shapes=[
            pltpu.VMEM((rows, columns), F32),
            pltpu.VMEM((rows, HD), F32),
            pltpu.VMEM((rows, HD), F32),
            pltpu.SemaphoreType.DMA,
            pltpu.SemaphoreType.DMA,
        ],
        compiler_params=pltpu.CompilerParams(
            collective_id=1, has_side_effects=True, vmem_limit_bytes=40 * 1024 * 1024
        ),
        cost_estimate=pl.CostEstimate(
            flops=2 * rows * columns * weight.shape[0],
            bytes_accessed=12_000_000,
            transcendentals=rows,
        ),
        name="project_norm",
    )(att, weight, stream, shift_mod, scale_mod)


def on_device(query, key, value, stream, shift_mod, scale_mod, out_weight):
    layers = lax.axis_size("seq") // HT
    weight = lax.all_gather(out_weight, "seq", axis=0, tiled=True)
    att = attention(query, key, value, layers, lax.axis_size("head"))
    return project(att, weight, stream, shift_mod[None, :], scale_mod[None, :])


def solution(mesh):
    return jax.shard_map(
        on_device,
        mesh=mesh,
        in_specs=(
            P(("video", "seq"), "head"),
            P(("video", "seq"), "head"),
            P(("video", "seq"), "head"),
            P(("video", "seq"), "head"),
            P("video"),
            P("video"),
            P("seq", "head"),
        ),
        out_specs=(P(("video", "seq"), "head"), P(("video", "seq"), "head")),
        check_vma=False,
    )
```

```python
import functools
import math

import jax
import jax.numpy as jnp
from jax import lax
from jax.experimental import pallas as pl
from jax.experimental.pallas import tpu as pltpu
from jax.sharding import PartitionSpec as P

HD = 128
TILE = 128
HT = 4
MESH = pl.DeviceIdType.MESH
F32 = jnp.float32
BF16 = jnp.bfloat16


def attention_kernel(
    layers, spans, chunk, ring, videos, q_ref, k_ref, v_ref, w_ref, out_ref, weight_ref,
    kbuf, vbuf, q_t, acc, top, total, send_sem, recv_sem, att_send, att_recv,
    ring_send, ring_recv, video_send, video_recv,
):
    rows, features = q_ref.shape
    chunks = features // chunk
    heads_chunk = chunk // HD
    width_tiles = rows // TILE
    position = lax.axis_index("seq")
    core = lax.axis_index("head")
    time = position // HT
    height = position % HT
    base = time * HT
    edge = (height == 0) | (height == HT - 1)
    inner = jnp.logical_not(edge)
    partner = base + height + 1 - 2 * (height % 2)
    far = base + (height + 2) % HT
    links = []
    if layers == 2:
        links.append((1, position + HT - 2 * base, True, True))
    elif layers > 2:
        links.append((1, position - HT, time > 0, time < layers - 1))
        links.append((2, position + HT, time < layers - 1, time > 0))

    def guarded(condition, body):
        if condition is True:
            body()
        else:
            pl.when(condition)(body)

    video = lax.axis_index("video")
    shard, columns = w_ref.shape
    piece = columns // videos
    place = jnp.where(position % 2 == 0, position // 2, ring - 1 - position // 2)
    reach = ((ring - 1) // 2, ring // 2)

    def ring_device(index):
        index = (index + ring) % ring
        return jnp.where(index < ring // 2, 2 * index, 2 * (ring - 1 - index) + 1)

    def piece_cols(of):
        return pl.ds(pl.multiple_of(of * piece, piece), piece)

    def block(direction, distance, of):
        owner = ring_device(place - distance if direction == 0 else place + distance)
        return weight_ref.at[pl.ds(pl.multiple_of(owner * shard, shard), shard), piece_cols(of)]

    def ring_copy(direction, distance, first=False):
        there = block(direction, distance - 1, video)
        return pltpu.make_async_remote_copy(
            src_ref=w_ref.at[:, piece_cols(video)] if first else there, dst_ref=there,
            send_sem=ring_send.at[direction, distance - 1],
            recv_sem=ring_recv.at[direction, distance - 1],
            device_id={"seq": ring_device(place + 1 if direction == 0 else place - 1)},
            device_id_type=MESH,
        )

    def video_copy(direction, distance, ahead, of):
        there = block(direction, distance, of)
        return pltpu.make_async_remote_copy(
            src_ref=there, dst_ref=there,
            send_sem=video_send.at[ahead - 1, direction, distance - 1],
            recv_sem=video_recv.at[ahead - 1, direction, distance - 1],
            device_id={"video": lax.rem(video + ahead, videos)}, device_id_type=MESH,
        )

    def ring_arrived(direction, distance):
        there = block(direction, distance, video)
        pltpu.make_async_remote_copy(
            src_ref=there, dst_ref=there,
            send_sem=ring_send.at[direction, distance - 1],
            recv_sem=ring_recv.at[direction, distance - 1],
            device_id={"seq": ring_device(place + 1)}, device_id_type=MESH,
        ).wait_recv()

    def weight_step(distance):
        for direction in (1, 0):
            def body(direction=direction):
                ring_arrived(direction, distance)
                pl.when(distance < reach[direction])(
                    lambda: ring_copy(direction, distance + 1).start()
                )
                for ahead in range(1, videos):
                    video_copy(direction, distance, ahead, video).start()
            pl.when(distance <= reach[direction])(body)

    def weight_drain(distance):
        for direction in (1, 0):
            def body(direction=direction):
                ring_copy(direction, distance).wait_send()
                for ahead in range(1, videos):
                    source = lax.rem(video + videos - ahead, videos)
                    video_copy(direction, distance, ahead, video).wait_send()
                    video_copy(direction, distance, ahead, source).wait_recv()
            pl.when(distance <= reach[direction])(body)

    barrier = pltpu.get_barrier_semaphore()

    def greet(device):
        pl.semaphore_signal(barrier, inc=1, device_id=device, device_id_type=MESH)

    greet({"seq": partner})
    greet({"seq": far})
    greet({"head": 1 - core})
    greet({"seq": ring_device(place + 1)})
    greet({"seq": ring_device(place - 1)})
    for ahead in range(1, videos):
        greet({"video": lax.rem(video + ahead, videos)})
    peers = 4 + videos
    for _, target, sends, _ in links:
        guarded(sends, lambda target=target: greet({"seq": target}))
        peers = peers + (1 if sends is True else jnp.where(sends, 1, 0))
    pl.semaphore_wait(barrier, peers)

    def cols(c):
        return pl.ds(pl.multiple_of(c * chunk, chunk), chunk)

    def copies(span, hop, c, target, crossed=False):
        pair = []
        for which, (own, buf) in enumerate(((k_ref, kbuf), (v_ref, vbuf))):
            dst = buf.at[span, hop, :, cols(c)]
            if hop == 2:
                src = buf.at[span, 3 if crossed else 1, :, cols(c)]
            elif span > 0 and hop > 0:
                src = buf.at[span, 0, :, cols(c)]
            else:
                src = own.at[:, cols(c)]
            pair.append(pltpu.make_async_remote_copy(
                src_ref=src, dst_ref=dst,
                send_sem=send_sem.at[which, span, hop, c],
                recv_sem=recv_sem.at[which, span, hop, c],
                device_id={"seq": target}, device_id_type=MESH,
            ))
        return pair

    def start(span, hop, c, target, crossed=False):
        for copy in copies(span, hop, c, target, crossed):
            copy.start()

    def is_crossed(c):
        return c % 3 == 1

    def start_own(span, c):
        start(span, 1, c, partner)
        pl.when(inner & is_crossed(c))(lambda: start(span, 3, c, far))

    def pass_straight(span, c):
        pl.when(edge & jnp.logical_not(is_crossed(c)))(lambda: start(span, 2, c, far))

    def pass_crossed(span, c):
        def body():
            arrived(span, 3, c)
            start(span, 2, c, partner, True)
        pl.when(edge & is_crossed(c))(body)

    def arrived(span, hop, c):
        for copy in copies(span, hop, c, partner):
            copy.wait_recv()

    def sent(span, hop, c, target):
        for copy in copies(span, hop, c, target):
            copy.wait_send()

    def first_sends(c, carry):
        for span, target, sends, _ in links:
            guarded(sends, lambda span=span, target=target: start(span, 0, c, target))
        start_own(0, c)
        return carry

    lax.fori_loop(0, chunks, first_sends, 0)
    for direction in (1, 0):
        if reach[direction] > 0:
            ring_copy(direction, 1, True).start()
    weight_ref[pl.ds(pl.multiple_of(position * shard, shard), shard), :] = w_ref[...]

    for head in range(features // HD):
        q_t[head] = q_ref[:, head * HD : (head + 1) * HD].astype(F32).T.astype(BF16)
    acc[...] = jnp.zeros_like(acc)
    total[...] = jnp.zeros_like(total)
    top[...] = jnp.full_like(top, -jnp.inf)
    factor = math.log2(math.e) / math.sqrt(HD)

    def attend(keys, values, c):
        def one_head(index, carry):
            head = c * heads_chunk + index
            here = pl.ds(pl.multiple_of(head * HD, HD), HD)
            scores = jnp.dot(keys[:, here], q_t[head], preferred_element_type=F32)
            old = top[head]
            parts, news, sums = [], [], []
            for tile in range(width_tiles):
                low = max(tile - 1, 0) * TILE
                high = min(tile + 2, width_tiles) * TILE
                at = slice(tile * TILE, (tile + 1) * TILE)
                seen = scores[low:high, at] * factor
                new = jnp.maximum(jnp.max(seen, axis=0, keepdims=True), old[:, at])
                expo = jnp.exp2(seen - new)
                sums.append(jnp.sum(expo, axis=0, keepdims=True))
                news.append(new)
                column = [expo.astype(BF16)]
                if low > 0:
                    column.insert(0, jnp.zeros((low, TILE), BF16))
                if high < rows:
                    column.append(jnp.zeros((rows - high, TILE), BF16))
                parts.append(jnp.concatenate(column, 0) if len(column) > 1 else column[0])
            probs = jnp.concatenate(parts, 1)
            new = jnp.concatenate(news, 1)
            scale = jnp.exp2(old - new)
            top[head] = new
            total[head] = total[head] * scale + jnp.concatenate(sums, 1)
            weighted = lax.dot_general(
                values[:, here], probs, (((0,), (0,)), ((), ())), preferred_element_type=F32
            )
            acc[head] = acc[head] * scale + weighted
            return carry

        lax.fori_loop(0, heads_chunk, one_head, 0)

    def attend_slot(span, hop, c):
        attend(kbuf.at[span, hop], vbuf.at[span, hop], c)

    def own_block(c, carry):
        attend(k_ref, v_ref, c)
        return carry

    lax.fori_loop(0, chunks, own_block, 0)

    valid = [(0, True)] + [(span, has) for span, _, _, has in links]

    def far_blocks(c):
        for span, has in valid:
            def body(span=span):
                arrived(span, 2, c)
                attend_slot(span, 2, c)
            guarded(inner if has is True else inner & has, body)

    def step(c, carry):
        arrived(0, 1, c)
        pass_straight(0, c)
        pass_crossed(0, c)
        for span, has in valid[1:]:
            def body(span=span):
                arrived(span, 0, c)
                start_own(span, c)
            guarded(has, body)
        attend_slot(0, 1, c)
        for span, has in valid[1:]:
            guarded(has, lambda span=span: attend_slot(span, 0, c))
        for span, has in valid[1:]:
            def body(span=span):
                arrived(span, 1, c)
                pass_straight(span, c)
                pass_crossed(span, c)
                attend_slot(span, 1, c)
            guarded(has, body)
        pl.when(c > 0)(lambda: far_blocks(c - 1))
        pl.when(c < reach[1])(lambda: weight_step(c + 1))
        return carry

    lax.fori_loop(0, chunks, step, 0)

    def late_weights(c, carry):
        weight_step(c + 1)
        return carry

    if reach[1] > chunks:
        lax.fori_loop(chunks, reach[1], late_weights, 0)
    far_blocks(chunks - 1)

    for head in range(features // HD):
        done = acc[head] / total[head]
        out_ref[core, :, head * HD : (head + 1) * HD] = done.T.astype(BF16)
    across = pltpu.make_async_remote_copy(
        src_ref=out_ref.at[core], dst_ref=out_ref.at[core],
        send_sem=att_send, recv_sem=att_recv,
        device_id={"head": 1 - core}, device_id_type=MESH,
    )
    across.start()

    def drain(c, carry):
        for span, target, sends, _ in links:
            guarded(sends, lambda span=span, target=target: sent(span, 0, c, target))
        for span, has in valid:
            def body(span=span):
                sent(span, 1, c, partner)
                pl.when(edge)(lambda: sent(span, 2, c, far))
                pl.when(inner & is_crossed(c))(lambda: sent(span, 3, c, far))
            guarded(has, body)
        return carry

    lax.fori_loop(0, chunks, drain, 0)

    def drain_weights(c, carry):
        weight_drain(c + 1)
        return carry

    lax.fori_loop(0, reach[1], drain_weights, 0)
    across.wait_send()
    arrive = pltpu.make_async_remote_copy(
        src_ref=out_ref.at[1 - core], dst_ref=out_ref.at[1 - core],
        send_sem=att_send, recv_sem=att_recv,
        device_id={"head": 1 - core}, device_id_type=MESH,
    )
    arrive.wait_recv()


def attention(query, key, value, out_weight, layers, heads_axis, ring, videos):
    rows, features = query.shape
    heads = features // HD
    chunk = HD
    chunks = features // chunk
    spans = min(layers, 3)
    shard, columns = out_weight.shape
    hops = ring // 2
    vmem = pl.BlockSpec(memory_space=pltpu.VMEM)
    return pl.pallas_call(
        functools.partial(attention_kernel, layers, spans, chunk, ring, videos),
        out_shape=(
            jax.ShapeDtypeStruct((heads_axis, rows, features), BF16),
            jax.ShapeDtypeStruct((ring * shard, columns), BF16),
        ),
        in_specs=[vmem] * 4,
        out_specs=(vmem, vmem),
        scratch_shapes=[
            pltpu.VMEM((spans, 4, rows, features), BF16),
            pltpu.VMEM((spans, 4, rows, features), BF16),
            pltpu.VMEM((heads, HD, rows), BF16),
            pltpu.VMEM((heads, HD, rows), F32),
            pltpu.VMEM((heads, 1, rows), F32),
            pltpu.VMEM((heads, 1, rows), F32),
            pltpu.SemaphoreType.DMA((2, spans, 4, chunks)),
            pltpu.SemaphoreType.DMA((2, spans, 4, chunks)),
            pltpu.SemaphoreType.DMA,
            pltpu.SemaphoreType.DMA,
            pltpu.SemaphoreType.DMA((2, hops)),
            pltpu.SemaphoreType.DMA((2, hops)),
            pltpu.SemaphoreType.DMA((max(videos - 1, 1), 2, hops)),
            pltpu.SemaphoreType.DMA((max(videos - 1, 1), 2, hops)),
        ],
        compiler_params=pltpu.CompilerParams(
            collective_id=0, has_side_effects=True, vmem_limit_bytes=40 * 1024 * 1024
        ),
        cost_estimate=pl.CostEstimate(
            flops=4 * spans * 3 * rows * rows * features,
            bytes_accessed=100_000_000,
            transcendentals=spans * 3 * rows * rows * heads,
        ),
        name="tile_attention",
    )(query, key, value, out_weight)


def project_kernel(
    width, att_ref, weight_ref, stream_ref, shift_ref, scale_ref, normed_ref, stream_out_ref,
    mixed, mine, theirs, send_sem, recv_sem,
):
    rows, columns = stream_ref.shape
    parts, _, depth = att_ref.shape
    core = lax.axis_index("head")
    other = {"head": 1 - core}
    barrier = pltpu.get_barrier_semaphore()
    pl.semaphore_signal(barrier, inc=1, device_id=other, device_id_type=MESH)
    step = 2 * HD
    sums = jnp.zeros((rows, HD), F32)
    squares = jnp.zeros((rows, HD), F32)
    for begin in range(0, columns, step):
        at = slice(begin, begin + step)
        block = stream_ref[:, at].astype(F32)
        product = jnp.dot(att_ref[0], weight_ref[0:depth, at], preferred_element_type=F32)
        for part in range(1, parts):
            product += jnp.dot(
                att_ref[part], weight_ref[part * depth : (part + 1) * depth, at],
                preferred_element_type=F32,
            )
        block = block + product
        mixed[:, at] = block
        stream_out_ref[:, at] = block.astype(BF16)
        for inside in range(0, step, HD):
            piece = block[:, inside : inside + HD]
            sums += piece
            squares += piece * piece
    lane = lax.broadcasted_iota(jnp.int32, (rows, HD), 1)
    sum_here = jnp.sum(sums, axis=1, keepdims=True)
    square_here = jnp.sum(squares, axis=1, keepdims=True)
    mine[...] = jnp.where(lane < HD // 2, sum_here, square_here)
    pl.semaphore_wait(barrier, 1)
    copy = pltpu.make_async_remote_copy(
        src_ref=mine, dst_ref=theirs, send_sem=send_sem, recv_sem=recv_sem,
        device_id=other, device_id_type=MESH,
    )
    copy.start()
    copy.wait()
    both = theirs[...]
    mean = (sum_here + both[:, 0:1]) / width
    var = (square_here + both[:, HD - 1 : HD]) / width - mean * mean
    inverse = lax.rsqrt(var + 1e-06)
    for begin in range(0, columns, step):
        at = slice(begin, begin + step)
        here = pl.ds(pl.multiple_of(core * columns + begin, step), step)
        gain = 1.0 + scale_ref[:, here]
        normed_ref[:, at] = (
            (mixed[:, at] - mean) * inverse * gain + shift_ref[:, here]
        ).astype(BF16)


def project(att, weight, stream, shift_mod, scale_mod):
    rows, columns = stream.shape
    width = shift_mod.shape[1]
    vmem = pl.BlockSpec(memory_space=pltpu.VMEM)
    return pl.pallas_call(
        functools.partial(project_kernel, width),
        out_shape=(
            jax.ShapeDtypeStruct((rows, columns), BF16),
            jax.ShapeDtypeStruct((rows, columns), BF16),
        ),
        in_specs=[vmem] * 5,
        out_specs=(vmem, vmem),
        scratch_shapes=[
            pltpu.VMEM((rows, columns), F32),
            pltpu.VMEM((rows, HD), F32),
            pltpu.VMEM((rows, HD), F32),
            pltpu.SemaphoreType.DMA,
            pltpu.SemaphoreType.DMA,
        ],
        compiler_params=pltpu.CompilerParams(
            collective_id=1, has_side_effects=True, vmem_limit_bytes=40 * 1024 * 1024
        ),
        cost_estimate=pl.CostEstimate(
            flops=2 * rows * columns * weight.shape[0],
            bytes_accessed=12_000_000,
            transcendentals=rows,
        ),
        name="project_norm",
    )(att, weight, stream, shift_mod, scale_mod)


def on_device(query, key, value, stream, shift_mod, scale_mod, out_weight):
    layers = lax.axis_size("seq") // HT
    att, weight = attention(
        query, key, value, out_weight, layers,
        lax.axis_size("head"), lax.axis_size("seq"), lax.axis_size("video"),
    )
    return project(att, weight, stream, shift_mod[None, :], scale_mod[None, :])


def solution(mesh):
    return jax.shard_map(
        on_device,
        mesh=mesh,
        in_specs=(
            P(("video", "seq"), "head"),
            P(("video", "seq"), "head"),
            P(("video", "seq"), "head"),
            P(("video", "seq"), "head"),
            P("video"),
            P("video"),
            P("seq", "head"),
        ),
        out_specs=(P(("video", "seq"), "head"), P(("video", "seq"), "head")),
        check_vma=False,
    )
```

```python
import functools
import math

import jax
import jax.numpy as jnp
from jax import lax
from jax.experimental import pallas as pl
from jax.experimental.pallas import tpu as pltpu
from jax.sharding import PartitionSpec as P

HD = 128
TILE = 128
HT = 4
MESH = pl.DeviceIdType.MESH
F32 = jnp.float32
BF16 = jnp.bfloat16


def attention_kernel(
    layers, spans, chunk, ring, videos, q_ref, k_ref, v_ref, w_ref, out_ref, weight_ref,
    kbuf, vbuf, q_t, acc, top, total, send_sem, recv_sem, att_send, att_recv,
    ring_send, ring_recv, video_send, video_recv,
):
    rows, features = q_ref.shape
    chunks = features // chunk
    heads_chunk = chunk // HD
    width_tiles = rows // TILE
    position = lax.axis_index("seq")
    core = lax.axis_index("head")
    time = position // HT
    height = position % HT
    base = time * HT
    edge = (height == 0) | (height == HT - 1)
    inner = jnp.logical_not(edge)
    partner = base + height + 1 - 2 * (height % 2)
    far = base + (height + 2) % HT
    links = []
    if layers == 2:
        links.append((1, position + HT - 2 * base, True, True))
    elif layers > 2:
        links.append((1, position - HT, time > 0, time < layers - 1))
        links.append((2, position + HT, time < layers - 1, time > 0))

    def guarded(condition, body):
        if condition is True:
            body()
        else:
            pl.when(condition)(body)

    video = lax.axis_index("video")
    shard, columns = w_ref.shape
    piece = columns // videos
    place = jnp.where(position % 2 == 0, position // 2, ring - 1 - position // 2)
    reach = ((ring - 1) // 2, ring // 2)

    def ring_device(index):
        index = (index + ring) % ring
        return jnp.where(index < ring // 2, 2 * index, 2 * (ring - 1 - index) + 1)

    def piece_cols(of):
        return pl.ds(pl.multiple_of(of * piece, piece), piece)

    def block(direction, distance, of):
        owner = ring_device(place - distance if direction == 0 else place + distance)
        return weight_ref.at[pl.ds(pl.multiple_of(owner * shard, shard), shard), piece_cols(of)]

    def ring_copy(direction, distance, first=False):
        there = block(direction, distance - 1, video)
        return pltpu.make_async_remote_copy(
            src_ref=w_ref.at[:, piece_cols(video)] if first else there, dst_ref=there,
            send_sem=ring_send.at[direction, distance - 1],
            recv_sem=ring_recv.at[direction, distance - 1],
            device_id={"seq": ring_device(place + 1 if direction == 0 else place - 1)},
            device_id_type=MESH,
        )

    def video_copy(direction, distance, ahead, of):
        there = block(direction, distance, of)
        return pltpu.make_async_remote_copy(
            src_ref=there, dst_ref=there,
            send_sem=video_send.at[ahead - 1, direction, distance - 1],
            recv_sem=video_recv.at[ahead - 1, direction, distance - 1],
            device_id={"video": lax.rem(video + ahead, videos)}, device_id_type=MESH,
        )

    def ring_arrived(direction, distance):
        there = block(direction, distance, video)
        pltpu.make_async_remote_copy(
            src_ref=there, dst_ref=there,
            send_sem=ring_send.at[direction, distance - 1],
            recv_sem=ring_recv.at[direction, distance - 1],
            device_id={"seq": ring_device(place + 1)}, device_id_type=MESH,
        ).wait_recv()

    def weight_step(distance):
        for direction in (1, 0):
            def body(direction=direction):
                ring_arrived(direction, distance)
                pl.when(distance < reach[direction])(
                    lambda: ring_copy(direction, distance + 1).start()
                )
                for ahead in range(1, videos):
                    video_copy(direction, distance, ahead, video).start()
            pl.when(distance <= reach[direction])(body)

    def weight_drain(distance):
        for direction in (1, 0):
            def body(direction=direction):
                ring_copy(direction, distance).wait_send()
                for ahead in range(1, videos):
                    source = lax.rem(video + videos - ahead, videos)
                    video_copy(direction, distance, ahead, video).wait_send()
                    video_copy(direction, distance, ahead, source).wait_recv()
            pl.when(distance <= reach[direction])(body)

    barrier = pltpu.get_barrier_semaphore()

    def greet(device):
        pl.semaphore_signal(barrier, inc=1, device_id=device, device_id_type=MESH)

    greet({"seq": partner})
    greet({"seq": far})
    greet({"head": 1 - core})
    greet({"seq": ring_device(place + 1)})
    greet({"seq": ring_device(place - 1)})
    for ahead in range(1, videos):
        greet({"video": lax.rem(video + ahead, videos)})
    peers = 4 + videos
    for _, target, sends, _ in links:
        guarded(sends, lambda target=target: greet({"seq": target}))
        peers = peers + (1 if sends is True else jnp.where(sends, 1, 0))
    pl.semaphore_wait(barrier, peers)

    def cols(c):
        return pl.ds(pl.multiple_of(c * chunk, chunk), chunk)

    def copies(span, hop, c, target, crossed=False):
        pair = []
        for which, (own, buf) in enumerate(((k_ref, kbuf), (v_ref, vbuf))):
            dst = buf.at[span, hop, :, cols(c)]
            if hop == 2:
                src = buf.at[span, 3 if crossed else 1, :, cols(c)]
            elif span > 0 and hop > 0:
                src = buf.at[span, 0, :, cols(c)]
            else:
                src = own.at[:, cols(c)]
            pair.append(pltpu.make_async_remote_copy(
                src_ref=src, dst_ref=dst,
                send_sem=send_sem.at[which, span, hop, c],
                recv_sem=recv_sem.at[which, span, hop, c],
                device_id={"seq": target}, device_id_type=MESH,
            ))
        return pair

    def start(span, hop, c, target, crossed=False):
        for copy in copies(span, hop, c, target, crossed):
            copy.start()

    def is_crossed(c):
        return c % 3 == 1

    def start_own(span, c):
        start(span, 1, c, partner)
        pl.when(inner & is_crossed(c))(lambda: start(span, 3, c, far))

    def pass_straight(span, c):
        pl.when(edge & jnp.logical_not(is_crossed(c)))(lambda: start(span, 2, c, far))

    def pass_crossed(span, c):
        def body():
            arrived(span, 3, c)
            start(span, 2, c, partner, True)
        pl.when(edge & is_crossed(c))(body)

    def arrived(span, hop, c):
        for copy in copies(span, hop, c, partner):
            copy.wait_recv()

    def sent(span, hop, c, target):
        for copy in copies(span, hop, c, target):
            copy.wait_send()

    def first_sends(c, carry):
        for span, target, sends, _ in links:
            guarded(sends, lambda span=span, target=target: start(span, 0, c, target))
        start_own(0, c)
        return carry

    ahead_of = min(2, chunks)
    lax.fori_loop(0, ahead_of, first_sends, 0)
    for direction in (1, 0):
        if reach[direction] > 0:
            ring_copy(direction, 1, True).start()
    weight_ref[pl.ds(pl.multiple_of(position * shard, shard), shard), :] = w_ref[...]

    for head in range(features // HD):
        q_t[head] = q_ref[:, head * HD : (head + 1) * HD].astype(F32).T.astype(BF16)
    acc[...] = jnp.zeros_like(acc)
    total[...] = jnp.zeros_like(total)
    top[...] = jnp.full_like(top, -jnp.inf)
    factor = math.log2(math.e) / math.sqrt(HD)

    def attend(keys, values, c):
        def one_head(index, carry):
            head = c * heads_chunk + index
            here = pl.ds(pl.multiple_of(head * HD, HD), HD)
            scores = jnp.dot(keys[:, here], q_t[head], preferred_element_type=F32)
            old = top[head]
            parts, news, sums = [], [], []
            for tile in range(width_tiles):
                low = max(tile - 1, 0) * TILE
                high = min(tile + 2, width_tiles) * TILE
                at = slice(tile * TILE, (tile + 1) * TILE)
                seen = scores[low:high, at] * factor
                new = jnp.maximum(jnp.max(seen, axis=0, keepdims=True), old[:, at])
                expo = jnp.exp2(seen - new)
                sums.append(jnp.sum(expo, axis=0, keepdims=True))
                news.append(new)
                column = [expo.astype(BF16)]
                if low > 0:
                    column.insert(0, jnp.zeros((low, TILE), BF16))
                if high < rows:
                    column.append(jnp.zeros((rows - high, TILE), BF16))
                parts.append(jnp.concatenate(column, 0) if len(column) > 1 else column[0])
            probs = jnp.concatenate(parts, 1)
            new = jnp.concatenate(news, 1)
            scale = jnp.exp2(old - new)
            top[head] = new
            total[head] = total[head] * scale + jnp.concatenate(sums, 1)
            weighted = lax.dot_general(
                values[:, here], probs, (((0,), (0,)), ((), ())), preferred_element_type=F32
            )
            acc[head] = acc[head] * scale + weighted
            return carry

        lax.fori_loop(0, heads_chunk, one_head, 0)

    def attend_slot(span, hop, c):
        attend(kbuf.at[span, hop], vbuf.at[span, hop], c)

    def own_block(c, carry):
        attend(k_ref, v_ref, c)
        return carry

    lax.fori_loop(0, chunks, own_block, 0)

    valid = [(0, True)] + [(span, has) for span, _, _, has in links]

    def far_blocks(c):
        for span, has in valid:
            def body(span=span):
                arrived(span, 2, c)
                attend_slot(span, 2, c)
            guarded(inner if has is True else inner & has, body)

    def near_blocks(c):
        arrived(0, 1, c)
        pass_straight(0, c)
        for span, has in valid[1:]:
            def body(span=span):
                arrived(span, 0, c)
                start_own(span, c)
            guarded(has, body)
        pass_crossed(0, c)

        @pl.when(c + ahead_of < chunks)
        def _():
            first_sends(c + ahead_of, 0)

    def near_attend(c):
        attend_slot(0, 1, c)
        for span, has in valid[1:]:
            guarded(has, lambda span=span: attend_slot(span, 0, c))

    def passed_blocks(c):
        for span, has in valid[1:]:
            def body(span=span):
                arrived(span, 1, c)
                pass_straight(span, c)
                pass_crossed(span, c)
                attend_slot(span, 1, c)
            guarded(has, body)

    def step(c, carry):
        pl.when(c < chunks)(lambda: near_blocks(c))
        pl.when((c >= 1) & (c <= chunks))(lambda: passed_blocks(c - 1))
        pl.when(c < chunks)(lambda: near_attend(c))
        pl.when(c >= 2)(lambda: far_blocks(c - 2))
        pl.when((c >= 1) & (c <= reach[1]))(lambda: weight_step(c))
        return carry

    lax.fori_loop(0, chunks + 2, step, 0)

    def late_weights(c, carry):
        weight_step(c + 1)
        return carry

    if reach[1] > chunks + 1:
        lax.fori_loop(chunks + 1, reach[1], late_weights, 0)

    for head in range(features // HD):
        done = acc[head] / total[head]
        out_ref[core, :, head * HD : (head + 1) * HD] = done.T.astype(BF16)
    across = pltpu.make_async_remote_copy(
        src_ref=out_ref.at[core], dst_ref=out_ref.at[core],
        send_sem=att_send, recv_sem=att_recv,
        device_id={"head": 1 - core}, device_id_type=MESH,
    )
    across.start()

    def drain(c, carry):
        for span, target, sends, _ in links:
            guarded(sends, lambda span=span, target=target: sent(span, 0, c, target))
        for span, has in valid:
            def body(span=span):
                sent(span, 1, c, partner)
                pl.when(edge)(lambda: sent(span, 2, c, far))
                pl.when(inner & is_crossed(c))(lambda: sent(span, 3, c, far))
            guarded(has, body)
        return carry

    lax.fori_loop(0, chunks, drain, 0)

    def drain_weights(c, carry):
        weight_drain(c + 1)
        return carry

    lax.fori_loop(0, reach[1], drain_weights, 0)
    across.wait_send()
    arrive = pltpu.make_async_remote_copy(
        src_ref=out_ref.at[1 - core], dst_ref=out_ref.at[1 - core],
        send_sem=att_send, recv_sem=att_recv,
        device_id={"head": 1 - core}, device_id_type=MESH,
    )
    arrive.wait_recv()


def attention(query, key, value, out_weight, layers, heads_axis, ring, videos):
    rows, features = query.shape
    heads = features // HD
    chunk = HD
    chunks = features // chunk
    spans = min(layers, 3)
    shard, columns = out_weight.shape
    hops = ring // 2
    vmem = pl.BlockSpec(memory_space=pltpu.VMEM)
    return pl.pallas_call(
        functools.partial(attention_kernel, layers, spans, chunk, ring, videos),
        out_shape=(
            jax.ShapeDtypeStruct((heads_axis, rows, features), BF16),
            jax.ShapeDtypeStruct((ring * shard, columns), BF16),
        ),
        in_specs=[vmem] * 4,
        out_specs=(vmem, vmem),
        scratch_shapes=[
            pltpu.VMEM((spans, 4, rows, features), BF16),
            pltpu.VMEM((spans, 4, rows, features), BF16),
            pltpu.VMEM((heads, HD, rows), BF16),
            pltpu.VMEM((heads, HD, rows), F32),
            pltpu.VMEM((heads, 1, rows), F32),
            pltpu.VMEM((heads, 1, rows), F32),
            pltpu.SemaphoreType.DMA((2, spans, 4, chunks)),
            pltpu.SemaphoreType.DMA((2, spans, 4, chunks)),
            pltpu.SemaphoreType.DMA,
            pltpu.SemaphoreType.DMA,
            pltpu.SemaphoreType.DMA((2, hops)),
            pltpu.SemaphoreType.DMA((2, hops)),
            pltpu.SemaphoreType.DMA((max(videos - 1, 1), 2, hops)),
            pltpu.SemaphoreType.DMA((max(videos - 1, 1), 2, hops)),
        ],
        compiler_params=pltpu.CompilerParams(
            collective_id=0, has_side_effects=True, vmem_limit_bytes=40 * 1024 * 1024
        ),
        cost_estimate=pl.CostEstimate(
            flops=4 * spans * 3 * rows * rows * features,
            bytes_accessed=100_000_000,
            transcendentals=spans * 3 * rows * rows * heads,
        ),
        name="tile_attention",
    )(query, key, value, out_weight)


def project_kernel(
    width, att_ref, weight_ref, stream_ref, shift_ref, scale_ref, normed_ref, stream_out_ref,
    mixed, mine, theirs, send_sem, recv_sem,
):
    rows, columns = stream_ref.shape
    parts, _, depth = att_ref.shape
    core = lax.axis_index("head")
    other = {"head": 1 - core}
    barrier = pltpu.get_barrier_semaphore()
    pl.semaphore_signal(barrier, inc=1, device_id=other, device_id_type=MESH)
    step = 2 * HD
    sums = jnp.zeros((rows, HD), F32)
    squares = jnp.zeros((rows, HD), F32)
    for begin in range(0, columns, step):
        at = slice(begin, begin + step)
        block = stream_ref[:, at].astype(F32)
        product = jnp.dot(att_ref[0], weight_ref[0:depth, at], preferred_element_type=F32)
        for part in range(1, parts):
            product += jnp.dot(
                att_ref[part], weight_ref[part * depth : (part + 1) * depth, at],
                preferred_element_type=F32,
            )
        block = block + product
        mixed[:, at] = block
        stream_out_ref[:, at] = block.astype(BF16)
        for inside in range(0, step, HD):
            piece = block[:, inside : inside + HD]
            sums += piece
            squares += piece * piece
    lane = lax.broadcasted_iota(jnp.int32, (rows, HD), 1)
    sum_here = jnp.sum(sums, axis=1, keepdims=True)
    square_here = jnp.sum(squares, axis=1, keepdims=True)
    mine[...] = jnp.where(lane < HD // 2, sum_here, square_here)
    pl.semaphore_wait(barrier, 1)
    copy = pltpu.make_async_remote_copy(
        src_ref=mine, dst_ref=theirs, send_sem=send_sem, recv_sem=recv_sem,
        device_id=other, device_id_type=MESH,
    )
    copy.start()
    copy.wait()
    both = theirs[...]
    mean = (sum_here + both[:, 0:1]) / width
    var = (square_here + both[:, HD - 1 : HD]) / width - mean * mean
    inverse = lax.rsqrt(var + 1e-06)
    for begin in range(0, columns, step):
        at = slice(begin, begin + step)
        here = pl.ds(pl.multiple_of(core * columns + begin, step), step)
        gain = 1.0 + scale_ref[:, here]
        normed_ref[:, at] = (
            (mixed[:, at] - mean) * inverse * gain + shift_ref[:, here]
        ).astype(BF16)


def project(att, weight, stream, shift_mod, scale_mod):
    rows, columns = stream.shape
    width = shift_mod.shape[1]
    vmem = pl.BlockSpec(memory_space=pltpu.VMEM)
    return pl.pallas_call(
        functools.partial(project_kernel, width),
        out_shape=(
            jax.ShapeDtypeStruct((rows, columns), BF16),
            jax.ShapeDtypeStruct((rows, columns), BF16),
        ),
        in_specs=[vmem] * 5,
        out_specs=(vmem, vmem),
        scratch_shapes=[
            pltpu.VMEM((rows, columns), F32),
            pltpu.VMEM((rows, HD), F32),
            pltpu.VMEM((rows, HD), F32),
            pltpu.SemaphoreType.DMA,
            pltpu.SemaphoreType.DMA,
        ],
        compiler_params=pltpu.CompilerParams(
            collective_id=1, has_side_effects=True, vmem_limit_bytes=40 * 1024 * 1024
        ),
        cost_estimate=pl.CostEstimate(
            flops=2 * rows * columns * weight.shape[0],
            bytes_accessed=12_000_000,
            transcendentals=rows,
        ),
        name="project_norm",
    )(att, weight, stream, shift_mod, scale_mod)


def on_device(query, key, value, stream, shift_mod, scale_mod, out_weight):
    layers = lax.axis_size("seq") // HT
    att, weight = attention(
        query, key, value, out_weight, layers,
        lax.axis_size("head"), lax.axis_size("seq"), lax.axis_size("video"),
    )
    return project(att, weight, stream, shift_mod[None, :], scale_mod[None, :])


def solution(mesh):
    return jax.shard_map(
        on_device,
        mesh=mesh,
        in_specs=(
            P(("video", "seq"), "head"),
            P(("video", "seq"), "head"),
            P(("video", "seq"), "head"),
            P(("video", "seq"), "head"),
            P("video"),
            P("video"),
            P("seq", "head"),
        ),
        out_specs=(P(("video", "seq"), "head"), P(("video", "seq"), "head")),
        check_vma=False,
    )
```
